32 devices in a mesh: wide: 16 (over z, x, core), row: 2 (over y).
Axes of the slice: x: 2, y: 2, z: 4, core: 2. Of those that a mesh axis runs over, the one named last changes fastest.
Arguments:
- points: float32 [128, 4096], P(None, ('wide', 'row')), may hold values from -6 to 6
- targets: float32 [32, 4096], P(None, ('wide', 'row')), may hold values from -6 to 6
- lengthscales: float32 [128], replicated, may hold values from 3.5 to 7
- outputscale: float32 [1], replicated, may hold values from 0.5 to 2
- noise: float32 [1], replicated, may hold values from 0.5 to 2
Outputs:
- solution: float32 [32, 4096], P(None, ('wide', 'row'))
- residual: float32 [32, 4096], P(None, ('wide', 'row'))
The draws below stay inside these ranges and needn't reach their ends.
All inputs are finite; a program needn't handle non-finite values.
Results may differ from the reference program's by a relative error of at most 0.0003.
Values sent between devices are 32-bit elements; how exact they have to be, the bound alone decides.
A program may use at most 64 MiB of HBM per device.

```python
import math
import jax
import jax.numpy as jnp
from jax import lax

D = 128
RHS = 32
ITERS = 2
POINTS = 4096
BLOCK = 256
N_WIDE = 16


def shard_levels(key, dims, shards, least, top_value):
    def one(axis_at, parts):
        heights = jax.random.uniform(jax.random.fold_in(jax.random.fold_in(key, 6), axis_at), (parts,), jnp.float32, least / len(shards), top_value / len(shards))
        return jnp.repeat(jnp.exp(heights), dims[axis_at] // parts).reshape((-1,) + (1,) * (len(dims) - axis_at - 1))

    gain = one(*shards[0])
    for cut in shards[1:]:
        gain = gain * one(*cut)
    return gain


def scatter_about(key, dims, width, limit, split=(), kind=jnp.bfloat16):
    values = jax.random.normal(key, dims, jnp.float32) * width
    if len(split) > 0:
        values = shard_levels(key, dims, split, -0.22, 0.18) * values
    return jnp.clip(values, min=-limit, max=limit).astype(kind)


def setup_inputs(seed: int = 0) -> dict:
    key_of = jax.random.split(jax.random.key(seed), 6)
    return {
        "points": scatter_about(key_of[0], (D, POINTS), 1.0, 6.0, ((1, 32),), jnp.float32),
        "targets": scatter_about(key_of[1], (RHS, POINTS), 1.0, 6.0, ((1, 32),), jnp.float32),
        "lengthscales": jnp.clip(jnp.exp(jax.random.uniform(key_of[2], (D,), jnp.float32, math.log(3.5), math.log(7.0))), 3.5, 7.0),
        "outputscale": jnp.clip(jnp.exp(jax.random.uniform(key_of[3], (1,), jnp.float32, math.log(0.5), math.log(2.0))), 0.5, 2.0),
        "noise": jnp.clip(jnp.exp(jax.random.uniform(key_of[4], (1,), jnp.float32, math.log(0.5), math.log(2.0))), 0.5, 2.0),
    }


def kernel_rows(scaled, squares, vectors, kern_scale, start):
    left_pts = lax.dynamic_slice_in_dim(scaled, start, BLOCK, 1)
    left_sq = lax.dynamic_slice_in_dim(squares, start, BLOCK, 0)
    cross = lax.dot_general(left_pts, scaled, (((0,), (0,)), ((), ())), precision=lax.Precision.HIGHEST)
    distance = left_sq[:, None] + squares[None, :] - 2.0 * cross
    kernel = kern_scale * jnp.exp(-0.5 * distance)
    return lax.dot_general(vectors, kernel, (((1,), (1,)), ((), ())), precision=lax.Precision.HIGHEST)


def operate(scaled, squares, vectors, kern_scale, noise_var):
    starts = (jnp.arange(N_WIDE) * BLOCK).astype(jnp.int32)
    pieces = lax.map(lambda start: kernel_rows(scaled, squares, vectors, kern_scale, start), starts)
    return pieces.transpose(1, 0, 2).reshape(RHS, POINTS) + noise_var * vectors


def reference(points, targets, lengthscales, outputscale, noise):
    scaled = points / lengthscales[:, None]
    squares = jnp.sum(scaled * scaled, axis=0)
    kern_scale = outputscale[0]
    noise_var = noise[0]
    solution = jnp.zeros_like(targets)
    residual = targets
    direction = targets
    norm_now = jnp.sum(residual * residual, axis=1)
    for iteration in range(ITERS):
        image = operate(scaled, squares, direction, kern_scale, noise_var)
        step_size = norm_now / jnp.sum(direction * image, axis=1)
        solution = solution + step_size[:, None] * direction
        residual = residual - step_size[:, None] * image
        norm_next = jnp.sum(residual * residual, axis=1)
        direction = residual + (norm_next / norm_now)[:, None] * direction
        norm_now = norm_next
    return solution, residual
```

```python
import functools

import jax
import jax.numpy as jnp
from jax import lax
from jax.experimental import pallas as pl
from jax.experimental.pallas import tpu as pltpu
from jax.sharding import PartitionSpec as P

ITERS = 2


def from_behind(value, axis, steps):
    count = lax.axis_size(axis)
    pairs = [(source, (source + steps) % count) for source in range(count)]
    return lax.ppermute(value, axis, pairs)


def kernel_tile(left_pts, left_sq, right_pts, right_sq, kern_scale):
    cross = lax.dot_general(
        left_pts, right_pts, (((0,), (0,)), ((), ())), precision=lax.Precision.HIGHEST
    )
    distance = left_sq[:, None] + right_sq[None, :] - 2.0 * cross
    return kern_scale * jnp.exp(-0.5 * distance)


def apply_rows(vectors, kernel):
    return lax.dot_general(
        vectors, kernel, (((1,), (1,)), ((), ())), precision=lax.Precision.HIGHEST
    )


def apply_columns(vectors, kernel):
    return lax.dot_general(
        vectors, kernel, (((1,), (0,)), ((), ())), precision=lax.Precision.HIGHEST
    )


def on_device(points, targets, lengthscales, outputscale, noise):
    wide_count = lax.axis_size("wide")
    row_count = lax.axis_size("row")
    half_cycle = wide_count // 2
    slot_count = half_cycle // row_count
    member = lax.axis_index("row")
    scaled = points / lengthscales[:, None]
    kern_scale = outputscale[0]
    noise_var = noise[0]
    features = scaled.shape[0]
    local_count = points.shape[1]

    def collect(stacked):
        window = stacked[None]
        while window.shape[0] < half_cycle:
            arrived = from_behind(window, "wide", -window.shape[0])
            window = jnp.concatenate([window, arrived], axis=0)
        return window

    def assemble(stacked):
        across = from_behind(stacked, "wide", -half_cycle)
        table = collect(stacked)
        channels = table.shape[1]
        nearer = table.reshape(slot_count, row_count, channels, local_count).transpose(0, 2, 1, 3)
        own_block = jnp.broadcast_to(
            table[0][None, :, None, :], (1, channels, row_count, local_count)
        )
        outgoing = jnp.concatenate([own_block, nearer], axis=0)
        arrived = lax.all_to_all(outgoing, "row", split_axis=2, concat_axis=2, tiled=True)
        return (arrived.reshape(slot_count + 1, channels, row_count * local_count), across)

    solution = jnp.zeros_like(targets)
    residual = targets
    direction = targets
    norm_now = lax.psum(jnp.sum(residual * residual, axis=1), ("wide", "row"))
    cache = None
    for iteration in range(ITERS):
        operate_cache = cache
        if operate_cache is None:
            blocks, operate_across = assemble(jnp.concatenate([scaled, direction], axis=0))
            point_blocks = blocks[:, :features]
            vector_blocks = blocks[:, features:]
            far_points = operate_across[:features]
            far_vector = operate_across[features:]
            operate_cache = (
                point_blocks,
                jnp.sum(point_blocks * point_blocks, axis=1),
                far_points,
                jnp.sum(far_points * far_points, axis=0),
            )
        else:
            vector_blocks, far_vector = assemble(direction)
        point_blocks, block_sq, far_points, far_sq = operate_cache
        left_pts = point_blocks[0]
        left_sq = block_sq[0]
        left_vec = vector_blocks[0]
        kernel = kernel_tile(left_pts, left_sq, far_points, far_sq, kern_scale)
        own_rows = apply_rows(far_vector, kernel)
        operate_partials = []
        for slot_index in range(slot_count):
            kernel = kernel_tile(
                left_pts,
                left_sq,
                point_blocks[slot_index + 1],
                block_sq[slot_index + 1],
                kern_scale,
            )
            own_rows = own_rows + apply_rows(vector_blocks[slot_index + 1], kernel)
            weight = (member + row_count * slot_index != 0).astype(jnp.float32)
            operate_partials.append(weight * apply_columns(left_vec, kernel))
        partials = jnp.stack([own_rows] + operate_partials, axis=0)
        rhs_count = partials.shape[1]
        pieces = partials.reshape(slot_count + 1, rhs_count, row_count, local_count)
        spread_arrived = lax.all_to_all(pieces, "row", split_axis=2, concat_axis=2, tiled=True)
        mine = jnp.sum(spread_arrived[0], axis=1)
        by_distance = (
            spread_arrived[1:].transpose(0, 2, 1, 3).reshape(half_cycle, rhs_count, local_count)
        )
        by_distance = by_distance.at[0].add(mine)
        held = by_distance
        span_size = half_cycle
        while span_size > 1:
            span_size = span_size // 2
            held = held[:span_size] + from_behind(held[span_size:], "wide", span_size)
        summed = held[0]
        image = summed + noise_var * direction
        cache = operate_cache
        curve, cross_term, image_sq = lax.psum(
            (
                jnp.sum(direction * image, axis=1),
                jnp.sum(residual * image, axis=1),
                jnp.sum(image * image, axis=1),
            ),
            ("wide", "row"),
        )
        step_size = norm_now / curve
        norm_next = norm_now - 2.0 * step_size * cross_term + step_size * step_size * image_sq
        solution = solution + step_size[:, None] * direction
        residual = residual - step_size[:, None] * image
        if iteration + 1 < ITERS:
            direction = residual + (norm_next / norm_now)[:, None] * direction
            norm_now = norm_next
    return (solution, residual)


MESH = pl.DeviceIdType.MESH
VMEM_BUDGET = 48 * 2**20
CORES = 2
SIDE = 2


def flip(index, mask):
    bit = 1
    while bit <= mask:
        if mask & bit:
            index = index + bit - 2 * bit * lax.rem(lax.div(index, bit), 2)
        bit *= 2
    return index


def halves(value):
    high = value.astype(jnp.bfloat16)
    low = (value - high.astype(jnp.float32)).astype(jnp.bfloat16)
    return high, low


def column_sums(value):
    return jnp.sum(value, axis=1, keepdims=True)


def fused(
    depth,
    points_ref, targets_ref, lengths_ref, scale_ref, noise_ref,
    solution_ref, residual_ref,
    stack, images, kern_high, kern_low, left, acc, direct, sums, scalars,
    send_a, recv_a, send_b, recv_b, send_c, recv_c,
):
    features, local = points_ref.shape
    rhs = targets_ref.shape[0]
    wide, row = lax.axis_index("wide"), lax.axis_index("row")
    core = lax.rem(wide, CORES)
    x = lax.rem(lax.div(wide, CORES), SIDE)
    z = lax.div(wide, CORES * SIDE)

    def place(level, dx, dy, dc):
        at_z, at_x, at_y, at_c = flip(z, level), flip(x, dx), flip(row, dy), flip(core, dc)
        return ((at_z * SIDE + at_x) * CORES + at_c, at_y)

    def slot(level, dx, dy, dc):
        at_wide, at_row = place(level, dx, dy, dc)
        return at_wide * SIDE + at_row

    plane = [(dx, dy) for dx in range(SIDE) for dy in range(SIDE)]
    beside = [(dx, dy, dc) for dx, dy in plane for dc in range(CORES) if dx + dy + dc > 0]

    barrier = pltpu.get_barrier_semaphore()
    peers = [place(level, 0, 0, 0) for level in range(1, depth)] + [place(0, *p) for p in beside]
    for peer in peers:
        pl.semaphore_signal(barrier, inc=1, device_id=peer, device_id_type=MESH)

    lengths = jnp.broadcast_to(lengths_ref[...], (features, features)).T
    own = points_ref[...] / lengths[:, :local]
    mine = slot(0, 0, 0, 0)
    stack[mine, :features, :] = own
    stack[mine, features:, :] = targets_ref[...]
    pl.semaphore_wait(barrier, len(peers))

    def gather(buffer, sends, recvs, use):
        started = []

        def copy(from_slot, to, number):
            made = pltpu.make_async_remote_copy(
                src_ref=buffer.at[from_slot],
                dst_ref=buffer.at[from_slot],
                send_sem=sends.at[number],
                recv_sem=recvs.at[from_slot],
                device_id=to,
                device_id_type=MESH,
            )
            made.start()
            started.append(made)

        def arrived(at):
            pltpu.make_async_remote_copy(
                src_ref=buffer.at[at],
                dst_ref=buffer.at[at],
                send_sem=sends.at[0],
                recv_sem=recvs.at[at],
                device_id=place(0, 0, 0, 1),
                device_id_type=MESH,
            ).wait_recv()

        side_x, side_y, sibling = place(0, 1, 0, 0), place(0, 0, 1, 0), place(0, 0, 0, 1)
        for level in range(depth):
            base = level * 8
            here = slot(level, 0, 0, 0)
            if level > 0:
                arrived(here)
            copy(here, side_x, base)
            copy(here, side_y, base + 1)
            if level == 0:
                for other in range(1, depth):
                    copy(here, place(other, 0, 0, 0), depth * 8 + other)
            copy(here, sibling, base + 2)
            if level > 0:
                finish(level - 1, buffer, arrived, copy, use)
        finish(depth - 1, buffer, arrived, copy, use)
        return started

    def finish(level, buffer, arrived, copy, use):
        base = level * 8
        side_x, side_y, sibling = place(0, 1, 0, 0), place(0, 0, 1, 0), place(0, 0, 0, 1)
        from_x, from_y, from_d = slot(level, 1, 0, 0), slot(level, 0, 1, 0), slot(level, 1, 1, 0)
        arrived(from_x)
        if level % 2 == 0:
            copy(from_x, side_y, base + 3)
        copy(from_x, sibling, base + 4)
        arrived(from_y)
        if level % 2 == 1:
            copy(from_y, side_x, base + 3)
        copy(from_y, sibling, base + 5)
        arrived(from_d)
        copy(from_d, sibling, base + 6)
        use(level, 0)
        for dx, dy in plane:
            arrived(slot(level, dx, dy, 1))
        use(level, 1)

    own_t = own.T
    high, low = halves(own_t)
    left[:local, :features] = high
    left[:local, features:] = high
    left[local:, :features] = low
    left[local:, features:] = low
    own_sq = column_sums(own_t * own_t)
    kern_scale = scale_ref[0]
    noise_var = noise_ref[0]
    acc[...] = jnp.zeros_like(acc)

    def group(level, dc):
        return [slot(level, dx, dy, dc) for dx, dy in plane]

    def apply(vectors, first):
        total = None
        for at, vector in enumerate(vectors):
            vec_high, vec_low = halves(vector)
            tile_high, tile_low = kern_high[first + at], kern_low[first + at]
            part = lax.dot_general(
                jnp.concatenate([vec_high, vec_low], axis=1),
                jnp.concatenate([tile_high, tile_high], axis=1),
                (((1,), (1,)), ((), ())),
                preferred_element_type=jnp.float32,
            ) + lax.dot_general(
                vec_high, tile_low, (((1,), (1,)), ((), ())), preferred_element_type=jnp.float32
            )
            total = part if total is None else total + part
        return total

    def build(level, dc):
        first = (level * CORES + dc) * len(plane)
        slots = group(level, dc)
        for at, place_at in enumerate(slots):
            block = stack[place_at, :features, :]
            block_high, block_low = halves(block)
            product = jnp.dot(
                left[...],
                jnp.concatenate([block_high, block_low], axis=0),
                preferred_element_type=jnp.float32,
            )
            cross = product[:local] + product[local:]
            block_sq = jnp.sum(block * block, axis=0, keepdims=True)
            tile = kern_scale * jnp.exp(-0.5 * (own_sq + block_sq - 2.0 * cross))
            tile_high, tile_low = halves(tile)
            kern_high[first + at] = tile_high
            kern_low[first + at] = tile_low
        vectors = [stack[place_at, features:, :] for place_at in slots]
        acc[...] += apply(vectors, first)
        sums[0] += sum(vector * vector for vector in vectors)

    sums[...] = jnp.zeros_like(sums)
    copies = gather(stack, send_a, recv_a, build)
    targets = targets_ref[...]
    images[mine] = acc[...] + noise_var * targets

    def curve(level, dc):
        sums[1] += sum(
            stack[place_at, features:, :] * images[place_at] for place_at in group(level, dc)
        )

    copies += gather(images, send_b, recv_b, curve)
    norm_now = column_sums(sums[0])
    step_size = norm_now / column_sums(sums[1])
    wide_step = jnp.broadcast_to(step_size, (rhs, local))
    count = depth * CORES * len(plane)
    total = jnp.zeros((rhs, local), jnp.float32)
    order = [s for level in range(depth) for dc in range(CORES) for s in group(level, dc)]
    for at, place_at in enumerate(order):
        left_over = stack[place_at, features:, :] - wide_step * images[place_at]
        direct[at] = left_over
        total += left_over * left_over
    norm_next = column_sums(total)
    ratio = jnp.broadcast_to(norm_next / norm_now, (rhs, local))
    image = jnp.zeros((rhs, local), jnp.float32)
    for first in range(0, count, len(plane)):
        vectors = [
            direct[first + at] + ratio * stack[order[first + at], features:, :]
            for at in range(len(plane))
        ]
        image += apply(vectors, first)
    residual = targets - wide_step * images[mine]
    direction = residual + ratio * targets
    image += noise_var * direction

    padded = jnp.concatenate(
        [direction * image, jnp.zeros((local - rhs, local), jnp.float32)], axis=0
    )
    curves = jnp.broadcast_to(jnp.sum(padded.T, axis=0, keepdims=True), (8, local))

    def exchange(value, base, partners):
        curve_ref = scalars.at[base]
        curve_ref[...] = value
        made = []
        for at, partner in enumerate(partners):
            made.append(
                pltpu.make_async_remote_copy(
                    src_ref=curve_ref,
                    dst_ref=scalars.at[base + 1 + at],
                    send_sem=send_c.at[base + at],
                    recv_sem=recv_c.at[base + at],
                    device_id=partner,
                    device_id_type=MESH,
                )
            )
            made[-1].start()
        for at, one in enumerate(made):
            one.wait_recv()
            value = value + scalars.at[base + 1 + at][...]
        copies.extend(made)
        return value

    curves = exchange(curves, 0, [place(level, 0, 0, 0) for level in range(1, depth)])
    curves = exchange(curves, depth, [place(0, *p) for p in beside])
    spread = jnp.broadcast_to(curves[:1], (local, local)).T[:rhs]
    last_step = jnp.broadcast_to(norm_next, (rhs, local)) / spread
    solution_ref[...] = wide_step * targets + last_step * direction
    residual_ref[...] = residual - last_step * image
    for one in copies:
        one.wait_send()


def on_device_fused(points, targets, lengthscales, outputscale, noise):
    features, local = points.shape
    rhs = targets.shape[0]
    devices = lax.axis_size("wide") * lax.axis_size("row")
    depth = lax.axis_size("wide") // (CORES * SIDE)
    vmem, smem = pl.BlockSpec(memory_space=pltpu.VMEM), pl.BlockSpec(memory_space=pltpu.SMEM)
    own = jax.ShapeDtypeStruct((rhs, local), jnp.float32)
    peers = depth - 1 + 2 * SIDE * SIDE - 1
    dma = pltpu.SemaphoreType.DMA
    return pl.pallas_call(
        functools.partial(fused, depth),
        out_shape=(own, own),
        in_specs=[vmem, vmem, vmem, smem, smem],
        out_specs=(vmem, vmem),
        scratch_shapes=[
            pltpu.VMEM((devices, features + rhs, local), jnp.float32),
            pltpu.VMEM((devices, rhs, local), jnp.float32),
            pltpu.VMEM((devices, local, local), jnp.bfloat16),
            pltpu.VMEM((devices, local, local), jnp.bfloat16),
            pltpu.VMEM((2 * local, 2 * features), jnp.bfloat16),
            pltpu.VMEM((rhs, local), jnp.float32),
            pltpu.VMEM((devices, rhs, local), jnp.float32),
            pltpu.VMEM((2, rhs, local), jnp.float32),
            pltpu.VMEM((peers + 2, 8, local), jnp.float32),
            dma((9 * depth,)),
            dma((devices,)),
            dma((9 * depth,)),
            dma((devices,)),
            dma((peers + 2,)),
            dma((peers + 2,)),
        ],
        compiler_params=pltpu.CompilerParams(
            collective_id=0, has_side_effects=True, vmem_limit_bytes=VMEM_BUDGET
        ),
    )(points, targets, lengthscales[None, :], outputscale, noise)


def solution(mesh):
    sizes = dict(mesh.shape)
    devices = sizes["wide"] * sizes["row"]
    depth = sizes["wide"] // (CORES * SIDE)

    def whole(points, targets, lengthscales, outputscale, noise):
        features, count = points.shape
        rhs = targets.shape[0]
        local = count // devices
        held = 4 * count * (features + 3 * rhs + local)
        fits = (
            sizes["row"] == SIDE
            and sizes["wide"] == depth * CORES * SIDE
            and depth & (depth - 1) == 0
            and local == features
            and rhs <= local
            and 2 * held <= VMEM_BUDGET
        )
        own = P(None, ("wide", "row"))
        return jax.shard_map(
            on_device_fused if fits else on_device,
            mesh=mesh,
            in_specs=(own, own, P(), P(), P()),
            out_specs=(own, own),
            check_vma=False,
        )(points, targets, lengthscales, outputscale, noise)

    return whole
```

```python
import functools

import jax
import jax.numpy as jnp
from jax import lax
from jax.experimental import pallas as pl
from jax.experimental.pallas import tpu as pltpu
from jax.sharding import PartitionSpec as P

ITERS = 2


def from_behind(value, axis, steps):
    count = lax.axis_size(axis)
    pairs = [(source, (source + steps) % count) for source in range(count)]
    return lax.ppermute(value, axis, pairs)


def kernel_tile(left_pts, left_sq, right_pts, right_sq, kern_scale):
    cross = lax.dot_general(
        left_pts, right_pts, (((0,), (0,)), ((), ())), precision=lax.Precision.HIGHEST
    )
    distance = left_sq[:, None] + right_sq[None, :] - 2.0 * cross
    return kern_scale * jnp.exp(-0.5 * distance)


def apply_rows(vectors, kernel):
    return lax.dot_general(
        vectors, kernel, (((1,), (1,)), ((), ())), precision=lax.Precision.HIGHEST
    )


def apply_columns(vectors, kernel):
    return lax.dot_general(
        vectors, kernel, (((1,), (0,)), ((), ())), precision=lax.Precision.HIGHEST
    )


def on_device(points, targets, lengthscales, outputscale, noise):
    wide_count = lax.axis_size("wide")
    row_count = lax.axis_size("row")
    half_cycle = wide_count // 2
    slot_count = half_cycle // row_count
    member = lax.axis_index("row")
    scaled = points / lengthscales[:, None]
    kern_scale = outputscale[0]
    noise_var = noise[0]
    features = scaled.shape[0]
    local_count = points.shape[1]

    def collect(stacked):
        window = stacked[None]
        while window.shape[0] < half_cycle:
            arrived = from_behind(window, "wide", -window.shape[0])
            window = jnp.concatenate([window, arrived], axis=0)
        return window

    def assemble(stacked):
        across = from_behind(stacked, "wide", -half_cycle)
        table = collect(stacked)
        channels = table.shape[1]
        nearer = table.reshape(slot_count, row_count, channels, local_count).transpose(0, 2, 1, 3)
        own_block = jnp.broadcast_to(
            table[0][None, :, None, :], (1, channels, row_count, local_count)
        )
        outgoing = jnp.concatenate([own_block, nearer], axis=0)
        arrived = lax.all_to_all(outgoing, "row", split_axis=2, concat_axis=2, tiled=True)
        return (arrived.reshape(slot_count + 1, channels, row_count * local_count), across)

    solution = jnp.zeros_like(targets)
    residual = targets
    direction = targets
    norm_now = lax.psum(jnp.sum(residual * residual, axis=1), ("wide", "row"))
    cache = None
    for iteration in range(ITERS):
        operate_cache = cache
        if operate_cache is None:
            blocks, operate_across = assemble(jnp.concatenate([scaled, direction], axis=0))
            point_blocks = blocks[:, :features]
            vector_blocks = blocks[:, features:]
            far_points = operate_across[:features]
            far_vector = operate_across[features:]
            operate_cache = (
                point_blocks,
                jnp.sum(point_blocks * point_blocks, axis=1),
                far_points,
                jnp.sum(far_points * far_points, axis=0),
            )
        else:
            vector_blocks, far_vector = assemble(direction)
        point_blocks, block_sq, far_points, far_sq = operate_cache
        left_pts = point_blocks[0]
        left_sq = block_sq[0]
        left_vec = vector_blocks[0]
        kernel = kernel_tile(left_pts, left_sq, far_points, far_sq, kern_scale)
        own_rows = apply_rows(far_vector, kernel)
        operate_partials = []
        for slot_index in range(slot_count):
            kernel = kernel_tile(
                left_pts,
                left_sq,
                point_blocks[slot_index + 1],
                block_sq[slot_index + 1],
                kern_scale,
            )
            own_rows = own_rows + apply_rows(vector_blocks[slot_index + 1], kernel)
            weight = (member + row_count * slot_index != 0).astype(jnp.float32)
            operate_partials.append(weight * apply_columns(left_vec, kernel))
        partials = jnp.stack([own_rows] + operate_partials, axis=0)
        rhs_count = partials.shape[1]
        pieces = partials.reshape(slot_count + 1, rhs_count, row_count, local_count)
        spread_arrived = lax.all_to_all(pieces, "row", split_axis=2, concat_axis=2, tiled=True)
        mine = jnp.sum(spread_arrived[0], axis=1)
        by_distance = (
            spread_arrived[1:].transpose(0, 2, 1, 3).reshape(half_cycle, rhs_count, local_count)
        )
        by_distance = by_distance.at[0].add(mine)
        held = by_distance
        span_size = half_cycle
        while span_size > 1:
            span_size = span_size // 2
            held = held[:span_size] + from_behind(held[span_size:], "wide", span_size)
        summed = held[0]
        image = summed + noise_var * direction
        cache = operate_cache
        curve, cross_term, image_sq = lax.psum(
            (
                jnp.sum(direction * image, axis=1),
                jnp.sum(residual * image, axis=1),
                jnp.sum(image * image, axis=1),
            ),
            ("wide", "row"),
        )
        step_size = norm_now / curve
        norm_next = norm_now - 2.0 * step_size * cross_term + step_size * step_size * image_sq
        solution = solution + step_size[:, None] * direction
        residual = residual - step_size[:, None] * image
        if iteration + 1 < ITERS:
            direction = residual + (norm_next / norm_now)[:, None] * direction
            norm_now = norm_next
    return (solution, residual)


MESH = pl.DeviceIdType.MESH
VMEM_BUDGET = 48 * 2**20
CORES = 2
SIDE = 2


def flip(index, mask):
    bit = 1
    while bit <= mask:
        if mask & bit:
            index = index + bit - 2 * bit * lax.rem(lax.div(index, bit), 2)
        bit *= 2
    return index


def halves(value):
    high = value.astype(jnp.bfloat16)
    low = (value - high.astype(jnp.float32)).astype(jnp.bfloat16)
    return high, low


def column_sums(value):
    return jnp.sum(value, axis=1, keepdims=True)


def fused(
    depth,
    points_ref, targets_ref, lengths_ref, scale_ref, noise_ref,
    solution_ref, residual_ref,
    stack, images, kern_high, kern_low, left, acc, direct, sums, scalars,
    send_a, recv_a, send_b, recv_b, send_c, recv_c,
):
    features, local = points_ref.shape
    rhs = targets_ref.shape[0]
    wide, row = lax.axis_index("wide"), lax.axis_index("row")
    core = lax.rem(wide, CORES)
    x = lax.rem(lax.div(wide, CORES), SIDE)
    z = lax.div(wide, CORES * SIDE)

    def place(level, dx, dy, dc):
        at_z, at_x, at_y, at_c = flip(z, level), flip(x, dx), flip(row, dy), flip(core, dc)
        return ((at_z * SIDE + at_x) * CORES + at_c, at_y)

    def slot(level, dx, dy, dc):
        at_wide, at_row = place(level, dx, dy, dc)
        return at_wide * SIDE + at_row

    plane = [(dx, dy) for dx in range(SIDE) for dy in range(SIDE)]
    beside = [(dx, dy, dc) for dx, dy in plane for dc in range(CORES) if dx + dy + dc > 0]

    barrier = pltpu.get_barrier_semaphore()
    peers = [place(level, 0, 0, 0) for level in range(1, depth)] + [place(0, *p) for p in beside]
    for peer in peers:
        pl.semaphore_signal(barrier, inc=1, device_id=peer, device_id_type=MESH)

    lengths = jnp.broadcast_to(lengths_ref[...], (features, features)).T
    own = points_ref[...] / lengths[:, :local]
    mine = slot(0, 0, 0, 0)
    stack[mine, :features, :] = own
    stack[mine, features:, :] = targets_ref[...]
    pl.semaphore_wait(barrier, len(peers))

    def gather(buffer, sends, recvs, use):
        started = []

        def copy(from_slot, to, number):
            made = pltpu.make_async_remote_copy(
                src_ref=buffer.at[from_slot],
                dst_ref=buffer.at[from_slot],
                send_sem=sends.at[number],
                recv_sem=recvs.at[from_slot],
                device_id=to,
                device_id_type=MESH,
            )
            made.start()
            started.append(made)

        def arrived(at):
            pltpu.make_async_remote_copy(
                src_ref=buffer.at[at],
                dst_ref=buffer.at[at],
                send_sem=sends.at[0],
                recv_sem=recvs.at[at],
                device_id=place(0, 0, 0, 1),
                device_id_type=MESH,
            ).wait_recv()

        sibling = place(0, 0, 0, 1)
        across = [(dx, dy) for dx, dy in plane if dx + dy > 0]
        for level in range(depth):
            here = slot(level, 0, 0, 0)
            if level > 0:
                arrived(here)
            else:
                for other in range(1, depth):
                    copy(here, place(other, 0, 0, 0), depth * 8 + other)
            for at, (dx, dy) in enumerate(across):
                copy(here, place(0, dx, dy, 0), level * 8 + at)
            copy(here, sibling, level * 8 + 3)
        for level in range(depth):
            for at, (dx, dy) in enumerate(across):
                landed = slot(level, dx, dy, 0)
                arrived(landed)
                copy(landed, sibling, level * 8 + 4 + at)
            use(level, 0)
            for dx, dy in plane:
                arrived(slot(level, dx, dy, 1))
            use(level, 1)
        return started

    own_t = own.T
    high, low = halves(own_t)
    left[:local, :features] = high
    left[:local, features:] = high
    left[local:, :features] = low
    left[local:, features:] = low
    own_sq = column_sums(own_t * own_t)
    kern_scale = scale_ref[0]
    noise_var = noise_ref[0]
    acc[...] = jnp.zeros_like(acc)

    def group(level, dc):
        return [slot(level, dx, dy, dc) for dx, dy in plane]

    def apply(vectors, first):
        total = None
        for at, vector in enumerate(vectors):
            vec_high, vec_low = halves(vector)
            tile_high, tile_low = kern_high[first + at], kern_low[first + at]
            part = lax.dot_general(
                jnp.concatenate([vec_high, vec_low], axis=1),
                jnp.concatenate([tile_high, tile_high], axis=1),
                (((1,), (1,)), ((), ())),
                preferred_element_type=jnp.float32,
            ) + lax.dot_general(
                vec_high, tile_low, (((1,), (1,)), ((), ())), preferred_element_type=jnp.float32
            )
            total = part if total is None else total + part
        return total

    def build(level, dc):
        first = (level * CORES + dc) * len(plane)
        slots = group(level, dc)
        for at, place_at in enumerate(slots):
            block = stack[place_at, :features, :]
            block_high, block_low = halves(block)
            product = jnp.dot(
                left[...],
                jnp.concatenate([block_high, block_low], axis=0),
                preferred_element_type=jnp.float32,
            )
            cross = product[:local] + product[local:]
            block_sq = jnp.sum(block * block, axis=0, keepdims=True)
            tile = kern_scale * jnp.exp(-0.5 * (own_sq + block_sq - 2.0 * cross))
            tile_high, tile_low = halves(tile)
            kern_high[first + at] = tile_high
            kern_low[first + at] = tile_low
        vectors = [stack[place_at, features:, :] for place_at in slots]
        acc[...] += apply(vectors, first)
        sums[0] += sum(vector * vector for vector in vectors)

    sums[...] = jnp.zeros_like(sums)
    copies = gather(stack, send_a, recv_a, build)
    targets = targets_ref[...]
    images[mine] = acc[...] + noise_var * targets

    def curve(level, dc):
        sums[1] += sum(
            stack[place_at, features:, :] * images[place_at] for place_at in group(level, dc)
        )

    copies += gather(images, send_b, recv_b, curve)
    norm_now = column_sums(sums[0])
    step_size = norm_now / column_sums(sums[1])
    wide_step = jnp.broadcast_to(step_size, (rhs, local))
    count = depth * CORES * len(plane)
    total = jnp.zeros((rhs, local), jnp.float32)
    order = [s for level in range(depth) for dc in range(CORES) for s in group(level, dc)]
    for at, place_at in enumerate(order):
        left_over = stack[place_at, features:, :] - wide_step * images[place_at]
        direct[at] = left_over
        total += left_over * left_over
    norm_next = column_sums(total)
    ratio = jnp.broadcast_to(norm_next / norm_now, (rhs, local))
    image = jnp.zeros((rhs, local), jnp.float32)
    for first in range(0, count, len(plane)):
        vectors = [
            direct[first + at] + ratio * stack[order[first + at], features:, :]
            for at in range(len(plane))
        ]
        image += apply(vectors, first)
    residual = targets - wide_step * images[mine]
    direction = residual + ratio * targets
    image += noise_var * direction

    padded = jnp.concatenate(
        [direction * image, jnp.zeros((local - rhs, local), jnp.float32)], axis=0
    )
    curves = jnp.broadcast_to(jnp.sum(padded.T, axis=0, keepdims=True), (8, local))

    def exchange(value, base, partners):
        curve_ref = scalars.at[base]
        curve_ref[...] = value
        made = []
        for at, partner in enumerate(partners):
            made.append(
                pltpu.make_async_remote_copy(
                    src_ref=curve_ref,
                    dst_ref=scalars.at[base + 1 + at],
                    send_sem=send_c.at[base + at],
                    recv_sem=recv_c.at[base + at],
                    device_id=partner,
                    device_id_type=MESH,
                )
            )
            made[-1].start()
        for at, one in enumerate(made):
            one.wait_recv()
            value = value + scalars.at[base + 1 + at][...]
        copies.extend(made)
        return value

    curves = exchange(curves, 0, [place(level, 0, 0, 0) for level in range(1, depth)])
    curves = exchange(curves, depth, [place(0, *p) for p in beside])
    spread = jnp.broadcast_to(curves[:1], (local, local)).T[:rhs]
    last_step = jnp.broadcast_to(norm_next, (rhs, local)) / spread
    solution_ref[...] = wide_step * targets + last_step * direction
    residual_ref[...] = residual - last_step * image
    for one in copies:
        one.wait_send()


def on_device_fused(points, targets, lengthscales, outputscale, noise):
    features, local = points.shape
    rhs = targets.shape[0]
    devices = lax.axis_size("wide") * lax.axis_size("row")
    depth = lax.axis_size("wide") // (CORES * SIDE)
    vmem, smem = pl.BlockSpec(memory_space=pltpu.VMEM), pl.BlockSpec(memory_space=pltpu.SMEM)
    own = jax.ShapeDtypeStruct((rhs, local), jnp.float32)
    peers = depth - 1 + 2 * SIDE * SIDE - 1
    dma = pltpu.SemaphoreType.DMA
    return pl.pallas_call(
        functools.partial(fused, depth),
        out_shape=(own, own),
        in_specs=[vmem, vmem, vmem, smem, smem],
        out_specs=(vmem, vmem),
        scratch_shapes=[
            pltpu.VMEM((devices, features + rhs, local), jnp.float32),
            pltpu.VMEM((devices, rhs, local), jnp.float32),
            pltpu.VMEM((devices, local, local), jnp.bfloat16),
            pltpu.VMEM((devices, local, local), jnp.bfloat16),
            pltpu.VMEM((2 * local, 2 * features), jnp.bfloat16),
            pltpu.VMEM((rhs, local), jnp.float32),
            pltpu.VMEM((devices, rhs, local), jnp.float32),
            pltpu.VMEM((2, rhs, local), jnp.float32),
            pltpu.VMEM((peers + 2, 8, local), jnp.float32),
            dma((9 * depth,)),
            dma((devices,)),
            dma((9 * depth,)),
            dma((devices,)),
            dma((peers + 2,)),
            dma((peers + 2,)),
        ],
        compiler_params=pltpu.CompilerParams(
            collective_id=0, has_side_effects=True, vmem_limit_bytes=VMEM_BUDGET
        ),
    )(points, targets, lengthscales[None, :], outputscale, noise)


def solution(mesh):
    sizes = dict(mesh.shape)
    devices = sizes["wide"] * sizes["row"]
    depth = sizes["wide"] // (CORES * SIDE)

    def whole(points, targets, lengthscales, outputscale, noise):
        features, count = points.shape
        rhs = targets.shape[0]
        local = count // devices
        held = 4 * count * (features + 3 * rhs + local)
        fits = (
            sizes["row"] == SIDE
            and sizes["wide"] == depth * CORES * SIDE
            and depth & (depth - 1) == 0
            and local == features
            and rhs <= local
            and 2 * held <= VMEM_BUDGET
        )
        own = P(None, ("wide", "row"))
        return jax.shard_map(
            on_device_fused if fits else on_device,
            mesh=mesh,
            in_specs=(own, own, P(), P(), P()),
            out_specs=(own, own),
            check_vma=False,
        )(points, targets, lengthscales, outputscale, noise)

    return whole
```

```python
import functools

import jax
import jax.numpy as jnp
from jax import lax
from jax.experimental import pallas as pl
from jax.experimental.pallas import tpu as pltpu
from jax.sharding import PartitionSpec as P

ITERS = 2


def from_behind(value, axis, steps):
    count = lax.axis_size(axis)
    pairs = [(source, (source + steps) % count) for source in range(count)]
    return lax.ppermute(value, axis, pairs)


def kernel_tile(left_pts, left_sq, right_pts, right_sq, kern_scale):
    cross = lax.dot_general(
        left_pts, right_pts, (((0,), (0,)), ((), ())), precision=lax.Precision.HIGHEST
    )
    distance = left_sq[:, None] + right_sq[None, :] - 2.0 * cross
    return kern_scale * jnp.exp(-0.5 * distance)


def apply_rows(vectors, kernel):
    return lax.dot_general(
        vectors, kernel, (((1,), (1,)), ((), ())), precision=lax.Precision.HIGHEST
    )


def apply_columns(vectors, kernel):
    return lax.dot_general(
        vectors, kernel, (((1,), (0,)), ((), ())), precision=lax.Precision.HIGHEST
    )


def on_device(points, targets, lengthscales, outputscale, noise):
    wide_count = lax.axis_size("wide")
    row_count = lax.axis_size("row")
    half_cycle = wide_count // 2
    slot_count = half_cycle // row_count
    member = lax.axis_index("row")
    scaled = points / lengthscales[:, None]
    kern_scale = outputscale[0]
    noise_var = noise[0]
    features = scaled.shape[0]
    local_count = points.shape[1]

    def collect(stacked):
        window = stacked[None]
        while window.shape[0] < half_cycle:
            arrived = from_behind(window, "wide", -window.shape[0])
            window = jnp.concatenate([window, arrived], axis=0)
        return window

    def assemble(stacked):
        across = from_behind(stacked, "wide", -half_cycle)
        table = collect(stacked)
        channels = table.shape[1]
        nearer = table.reshape(slot_count, row_count, channels, local_count).transpose(0, 2, 1, 3)
        own_block = jnp.broadcast_to(
            table[0][None, :, None, :], (1, channels, row_count, local_count)
        )
        outgoing = jnp.concatenate([own_block, nearer], axis=0)
        arrived = lax.all_to_all(outgoing, "row", split_axis=2, concat_axis=2, tiled=True)
        return (arrived.reshape(slot_count + 1, channels, row_count * local_count), across)

    solution = jnp.zeros_like(targets)
    residual = targets
    direction = targets
    norm_now = lax.psum(jnp.sum(residual * residual, axis=1), ("wide", "row"))
    cache = None
    for iteration in range(ITERS):
        operate_cache = cache
        if operate_cache is None:
            blocks, operate_across = assemble(jnp.concatenate([scaled, direction], axis=0))
            point_blocks = blocks[:, :features]
            vector_blocks = blocks[:, features:]
            far_points = operate_across[:features]
            far_vector = operate_across[features:]
            operate_cache = (
                point_blocks,
                jnp.sum(point_blocks * point_blocks, axis=1),
                far_points,
                jnp.sum(far_points * far_points, axis=0),
            )
        else:
            vector_blocks, far_vector = assemble(direction)
        point_blocks, block_sq, far_points, far_sq = operate_cache
        left_pts = point_blocks[0]
        left_sq = block_sq[0]
        left_vec = vector_blocks[0]
        kernel = kernel_tile(left_pts, left_sq, far_points, far_sq, kern_scale)
        own_rows = apply_rows(far_vector, kernel)
        operate_partials = []
        for slot_index in range(slot_count):
            kernel = kernel_tile(
                left_pts,
                left_sq,
                point_blocks[slot_index + 1],
                block_sq[slot_index + 1],
                kern_scale,
            )
            own_rows = own_rows + apply_rows(vector_blocks[slot_index + 1], kernel)
            weight = (member + row_count * slot_index != 0).astype(jnp.float32)
            operate_partials.append(weight * apply_columns(left_vec, kernel))
        partials = jnp.stack([own_rows] + operate_partials, axis=0)
        rhs_count = partials.shape[1]
        pieces = partials.reshape(slot_count + 1, rhs_count, row_count, local_count)
        spread_arrived = lax.all_to_all(pieces, "row", split_axis=2, concat_axis=2, tiled=True)
        mine = jnp.sum(spread_arrived[0], axis=1)
        by_distance = (
            spread_arrived[1:].transpose(0, 2, 1, 3).reshape(half_cycle, rhs_count, local_count)
        )
        by_distance = by_distance.at[0].add(mine)
        held = by_distance
        span_size = half_cycle
        while span_size > 1:
            span_size = span_size // 2
            held = held[:span_size] + from_behind(held[span_size:], "wide", span_size)
        summed = held[0]
        image = summed + noise_var * direction
        cache = operate_cache
        curve, cross_term, image_sq = lax.psum(
            (
                jnp.sum(direction * image, axis=1),
                jnp.sum(residual * image, axis=1),
                jnp.sum(image * image, axis=1),
            ),
            ("wide", "row"),
        )
        step_size = norm_now / curve
        norm_next = norm_now - 2.0 * step_size * cross_term + step_size * step_size * image_sq
        solution = solution + step_size[:, None] * direction
        residual = residual - step_size[:, None] * image
        if iteration + 1 < ITERS:
            direction = residual + (norm_next / norm_now)[:, None] * direction
            norm_now = norm_next
    return (solution, residual)


MESH = pl.DeviceIdType.MESH
VMEM_BUDGET = 48 * 2**20
CORES = 2
SIDE = 2


def flip(index, mask):
    bit = 1
    while bit <= mask:
        if mask & bit:
            index = index + bit - 2 * bit * lax.rem(lax.div(index, bit), 2)
        bit *= 2
    return index


def halves(value):
    high = value.astype(jnp.bfloat16)
    low = (value - high.astype(jnp.float32)).astype(jnp.bfloat16)
    return high, low


def column_sums(value):
    return jnp.sum(value, axis=1, keepdims=True)


def fused(
    depth,
    points_ref, targets_ref, lengths_ref, scale_ref, noise_ref,
    solution_ref, residual_ref,
    stack, images, kern_high, kern_low, parts, landing, scalars,
    send_a, recv_a, send_b, recv_b, send_p, recv_p, send_s, recv_s,
):
    features, local = points_ref.shape
    rhs = targets_ref.shape[0]
    wide, row = lax.axis_index("wide"), lax.axis_index("row")
    core = lax.rem(wide, CORES)
    x = lax.rem(lax.div(wide, CORES), SIDE)
    z = lax.div(wide, CORES * SIDE)
    plane = [(dx, dy, dc) for dc in range(CORES) for dx in range(SIDE) for dy in range(SIDE)]
    across = [(dx, dy, 0) for dx in range(SIDE) for dy in range(SIDE) if dx + dy > 0]
    width = len(plane)
    everyone = [(level, *at) for level in range(depth) for at in plane][1:]

    def place(level, dx, dy, dc):
        at_z, at_x, at_y, at_c = flip(z, level), flip(x, dx), flip(row, dy), flip(core, dc)
        return ((at_z * SIDE + at_x) * CORES + at_c, at_y)

    def number(dx, dy, dc):
        return plane.index((dx, dy, dc))

    barrier = pltpu.get_barrier_semaphore()
    for peer in everyone:
        pl.semaphore_signal(barrier, inc=1, device_id=place(*peer), device_id_type=MESH)

    lengths = jnp.broadcast_to(lengths_ref[...], (features, features)).T
    targets = targets_ref[...]
    stack[0, :features, :] = points_ref[...] / lengths[:, :local]
    stack[0, features:, :] = targets
    images[0] = jnp.zeros_like(targets)
    pl.semaphore_wait(barrier, len(everyone))

    started = []

    def copy(source, target, sends, sent, recvs, received, to):
        made = pltpu.make_async_remote_copy(
            src_ref=source,
            dst_ref=target,
            send_sem=sends.at[sent],
            recv_sem=recvs.at[received],
            device_id=place(*to),
            device_id_type=MESH,
        )
        made.start()
        started.append(made)
        return made

    def spread(buffer, sends, recvs):
        column, beside = {}, {}
        for level in range(1, depth):
            at = width + level - 1
            column[level] = copy(buffer.at[0], buffer.at[at], sends, at, recvs, at, (level, 0, 0, 0))
        for to in across:
            at = number(*to)
            beside[to] = copy(buffer.at[0], buffer.at[at], sends, at, recvs, at, (0, *to))
        at = number(0, 0, 1)
        beside[0, 0, 1] = copy(buffer.at[0], buffer.at[at], sends, at, recvs, at, (0, 0, 0, 1))
        return column, beside

    def relay(buffer, sends, recvs, beside):
        for to in across:
            beside[to].wait_recv()
            at = number(to[0], to[1], 1)
            beside[to[0], to[1], 1] = copy(
                buffer.at[number(*to)], buffer.at[at], sends, at, recvs, at, (0, 0, 0, 1)
            )
        for at in plane[SIDE * SIDE :]:
            beside[at].wait_recv()

    kern_scale = scale_ref[0]
    noise_var = noise_ref[0]

    def apply(vectors, level):
        total = None
        for at, (vec_high, vec_low) in enumerate(vectors):
            tile_high, tile_low = kern_high[level * width + at], kern_low[level * width + at]
            part = lax.dot_general(
                jnp.concatenate([vec_high, vec_low], axis=1),
                jnp.concatenate([tile_high, tile_high], axis=1),
                (((1,), (1,)), ((), ())),
                preferred_element_type=jnp.float32,
            ) + lax.dot_general(
                vec_high, tile_low, (((1,), (1,)), ((), ())), preferred_element_type=jnp.float32
            )
            total = part if total is None else total + part
        return total

    def build(level):
        own = stack[0 if level == 0 else width + level - 1, :features, :].T
        own_sq = column_sums(own * own)
        high, low = halves(own)
        left = jnp.concatenate(
            [jnp.concatenate([high, high], axis=1), jnp.concatenate([low, low], axis=1)], axis=0
        )
        for at in range(width):
            block = stack[at, :features, :]
            block_high, block_low = halves(block)
            product = jnp.dot(
                left,
                jnp.concatenate([block_high, block_low], axis=0),
                preferred_element_type=jnp.float32,
            )
            cross = product[:local] + product[local:]
            block_sq = jnp.sum(block * block, axis=0, keepdims=True)
            tile = kern_scale * jnp.exp(-0.5 * (own_sq + block_sq - 2.0 * cross))
            tile_high, tile_low = halves(tile)
            kern_high[level * width + at] = tile_high
            kern_low[level * width + at] = tile_low

    def send_part(turn, level, value):
        at = turn * depth + level
        parts[at] = value
        return copy(parts.at[at], landing.at[at], send_p, at, recv_p, at, (level, 0, 0, 0))

    def send_scalars(turn, values):
        pad = jnp.zeros((local - len(values) * rhs, local), jnp.float32)
        sums = jnp.sum(jnp.concatenate([*values, pad], axis=0).T, axis=0, keepdims=True)
        base = turn * (len(everyone) + 1)
        scalars[base] = jnp.broadcast_to(sums, scalars.shape[1:])
        return [
            copy(scalars.at[base], scalars.at[base + 1 + at], send_s, base + 1 + at, recv_s, base + 1 + at, peer)
            for at, peer in enumerate(everyone)
        ]

    def all_scalars(turn, copies):
        for one in copies:
            one.wait_recv()
        base = turn * (len(everyone) + 1)
        total = scalars[base]
        for at in range(len(everyone)):
            total = total + scalars[base + 1 + at]
        return jnp.broadcast_to(total[:1], (local, local)).T

    column, beside = spread(stack, send_a, recv_a)
    relay(stack, send_a, recv_a, beside)
    vectors = [halves(stack[at, features:, :]) for at in range(width)]
    build(0)
    mine = apply(vectors, 0)
    sent = []
    for level in range(1, depth):
        column[level].wait_recv()
        build(level)
        sent.append(send_part(0, level, apply(vectors, level)))
    for one in sent:
        one.wait_recv()
    for level in range(1, depth):
        mine = mine + landing[level]
    first_image = mine + noise_var * targets
    images[0] = first_image
    column, beside = spread(images, send_b, recv_b)
    sent = send_scalars(0, [targets * targets, targets * first_image, first_image * first_image])
    relay(images, send_b, recv_b, beside)
    for level in range(1, depth):
        column[level].wait_recv()
    found = all_scalars(0, sent)
    norm_now, curve, image_sq = found[:rhs], found[rhs : 2 * rhs], found[2 * rhs : 3 * rhs]
    step = norm_now / curve
    norm_next = norm_now - 2.0 * step * curve + step * step * image_sq
    ratio = norm_next / norm_now

    def turned(at):
        vector = stack[at, features:, :]
        return (vector - step * images[at]) + ratio * vector

    vectors = [halves(turned(at)) for at in range(width)]
    direction = turned(0)
    sent = []
    weighted = noise_var * direction * direction
    for level in range(1, depth):
        part = apply(vectors, level)
        sent.append(send_part(1, level, part))
        weighted += turned(width + level - 1) * part
    mine = apply(vectors, 0)
    weighted += direction * mine
    sums = send_scalars(1, [weighted])
    for one in sent:
        one.wait_recv()
    for level in range(1, depth):
        mine = mine + landing[depth + level]
    image = mine + noise_var * direction
    residual = targets - step * first_image
    last_step = norm_next / all_scalars(1, sums)[:rhs]
    solution_ref[...] = step * targets + last_step * direction
    residual_ref[...] = residual - last_step * image
    for one in started:
        one.wait_send()


def on_device_fused(points, targets, lengthscales, outputscale, noise):
    features, local = points.shape
    rhs = targets.shape[0]
    devices = lax.axis_size("wide") * lax.axis_size("row")
    depth = lax.axis_size("wide") // (CORES * SIDE)
    vmem, smem = pl.BlockSpec(memory_space=pltpu.VMEM), pl.BlockSpec(memory_space=pltpu.SMEM)
    own = jax.ShapeDtypeStruct((rhs, local), jnp.float32)
    width = SIDE * SIDE * CORES
    near = width + depth - 1
    dma = pltpu.SemaphoreType.DMA
    return pl.pallas_call(
        functools.partial(fused, depth),
        out_shape=(own, own),
        in_specs=[vmem, vmem, vmem, smem, smem],
        out_specs=(vmem, vmem),
        scratch_shapes=[
            pltpu.VMEM((near, features + rhs, local), jnp.float32),
            pltpu.VMEM((near, rhs, local), jnp.float32),
            pltpu.VMEM((depth * width, local, local), jnp.bfloat16),
            pltpu.VMEM((depth * width, local, local), jnp.bfloat16),
            pltpu.VMEM((2 * depth, rhs, local), jnp.float32),
            pltpu.VMEM((2 * depth, rhs, local), jnp.float32),
            pltpu.VMEM((2 * devices, 8, local), jnp.float32),
            dma((near,)),
            dma((near,)),
            dma((near,)),
            dma((near,)),
            dma((2 * depth,)),
            dma((2 * depth,)),
            dma((2 * devices,)),
            dma((2 * devices,)),
        ],
        compiler_params=pltpu.CompilerParams(
            collective_id=0, has_side_effects=True, vmem_limit_bytes=VMEM_BUDGET
        ),
    )(points, targets, lengthscales[None, :], outputscale, noise)


def solution(mesh):
    sizes = dict(mesh.shape)
    devices = sizes["wide"] * sizes["row"]
    depth = sizes["wide"] // (CORES * SIDE)

    def whole(points, targets, lengthscales, outputscale, noise):
        features, count = points.shape
        rhs = targets.shape[0]
        local = count // devices
        held = 4 * count * (features + 3 * rhs + local)
        fits = (
            sizes["row"] == SIDE
            and sizes["wide"] == depth * CORES * SIDE
            and depth & (depth - 1) == 0
            and local == features
            and 3 * rhs <= local
            and 2 * held <= VMEM_BUDGET
        )
        own = P(None, ("wide", "row"))
        return jax.shard_map(
            on_device_fused if fits else on_device,
            mesh=mesh,
            in_specs=(own, own, P(), P(), P()),
            out_specs=(own, own),
            check_vma=False,
        )(points, targets, lengthscales, outputscale, noise)

    return whole
```

```python
import functools

import jax
import jax.numpy as jnp
from jax import lax
from jax.experimental import pallas as pl
from jax.experimental.pallas import tpu as pltpu
from jax.sharding import PartitionSpec as P

ITERS = 2


def from_behind(value, axis, steps):
    count = lax.axis_size(axis)
    pairs = [(source, (source + steps) % count) for source in range(count)]
    return lax.ppermute(value, axis, pairs)


def kernel_tile(left_pts, left_sq, right_pts, right_sq, kern_scale):
    cross = lax.dot_general(
        left_pts, right_pts, (((0,), (0,)), ((), ())), precision=lax.Precision.HIGHEST
    )
    distance = left_sq[:, None] + right_sq[None, :] - 2.0 * cross
    return kern_scale * jnp.exp(-0.5 * distance)


def apply_rows(vectors, kernel):
    return lax.dot_general(
        vectors, kernel, (((1,), (1,)), ((), ())), precision=lax.Precision.HIGHEST
    )


def apply_columns(vectors, kernel):
    return lax.dot_general(
        vectors, kernel, (((1,), (0,)), ((), ())), precision=lax.Precision.HIGHEST
    )


def on_device(points, targets, lengthscales, outputscale, noise):
    wide_count = lax.axis_size("wide")
    row_count = lax.axis_size("row")
    half_cycle = wide_count // 2
    slot_count = half_cycle // row_count
    member = lax.axis_index("row")
    scaled = points / lengthscales[:, None]
    kern_scale = outputscale[0]
    noise_var = noise[0]
    features = scaled.shape[0]
    local_count = points.shape[1]

    def collect(stacked):
        window = stacked[None]
        while window.shape[0] < half_cycle:
            arrived = from_behind(window, "wide", -window.shape[0])
            window = jnp.concatenate([window, arrived], axis=0)
        return window

    def assemble(stacked):
        across = from_behind(stacked, "wide", -half_cycle)
        table = collect(stacked)
        channels = table.shape[1]
        nearer = table.reshape(slot_count, row_count, channels, local_count).transpose(0, 2, 1, 3)
        own_block = jnp.broadcast_to(
            table[0][None, :, None, :], (1, channels, row_count, local_count)
        )
        outgoing = jnp.concatenate([own_block, nearer], axis=0)
        arrived = lax.all_to_all(outgoing, "row", split_axis=2, concat_axis=2, tiled=True)
        return (arrived.reshape(slot_count + 1, channels, row_count * local_count), across)

    solution = jnp.zeros_like(targets)
    residual = targets
    direction = targets
    norm_now = lax.psum(jnp.sum(residual * residual, axis=1), ("wide", "row"))
    cache = None
    for iteration in range(ITERS):
        operate_cache = cache
        if operate_cache is None:
            blocks, operate_across = assemble(jnp.concatenate([scaled, direction], axis=0))
            point_blocks = blocks[:, :features]
            vector_blocks = blocks[:, features:]
            far_points = operate_across[:features]
            far_vector = operate_across[features:]
            operate_cache = (
                point_blocks,
                jnp.sum(point_blocks * point_blocks, axis=1),
                far_points,
                jnp.sum(far_points * far_points, axis=0),
            )
        else:
            vector_blocks, far_vector = assemble(direction)
        point_blocks, block_sq, far_points, far_sq = operate_cache
        left_pts = point_blocks[0]
        left_sq = block_sq[0]
        left_vec = vector_blocks[0]
        kernel = kernel_tile(left_pts, left_sq, far_points, far_sq, kern_scale)
        own_rows = apply_rows(far_vector, kernel)
        operate_partials = []
        for slot_index in range(slot_count):
            kernel = kernel_tile(
                left_pts,
                left_sq,
                point_blocks[slot_index + 1],
                block_sq[slot_index + 1],
                kern_scale,
            )
            own_rows = own_rows + apply_rows(vector_blocks[slot_index + 1], kernel)
            weight = (member + row_count * slot_index != 0).astype(jnp.float32)
            operate_partials.append(weight * apply_columns(left_vec, kernel))
        partials = jnp.stack([own_rows] + operate_partials, axis=0)
        rhs_count = partials.shape[1]
        pieces = partials.reshape(slot_count + 1, rhs_count, row_count, local_count)
        spread_arrived = lax.all_to_all(pieces, "row", split_axis=2, concat_axis=2, tiled=True)
        mine = jnp.sum(spread_arrived[0], axis=1)
        by_distance = (
            spread_arrived[1:].transpose(0, 2, 1, 3).reshape(half_cycle, rhs_count, local_count)
        )
        by_distance = by_distance.at[0].add(mine)
        held = by_distance
        span_size = half_cycle
        while span_size > 1:
            span_size = span_size // 2
            held = held[:span_size] + from_behind(held[span_size:], "wide", span_size)
        summed = held[0]
        image = summed + noise_var * direction
        cache = operate_cache
        curve, cross_term, image_sq = lax.psum(
            (
                jnp.sum(direction * image, axis=1),
                jnp.sum(residual * image, axis=1),
                jnp.sum(image * image, axis=1),
            ),
            ("wide", "row"),
        )
        step_size = norm_now / curve
        norm_next = norm_now - 2.0 * step_size * cross_term + step_size * step_size * image_sq
        solution = solution + step_size[:, None] * direction
        residual = residual - step_size[:, None] * image
        if iteration + 1 < ITERS:
            direction = residual + (norm_next / norm_now)[:, None] * direction
            norm_now = norm_next
    return (solution, residual)


MESH = pl.DeviceIdType.MESH
VMEM_BUDGET = 48 * 2**20
CORES = 2
SIDE = 2


def flip(index, mask):
    bit = 1
    while bit <= mask:
        if mask & bit:
            index = index + bit - 2 * bit * lax.rem(lax.div(index, bit), 2)
        bit *= 2
    return index


def halves(value):
    high = value.astype(jnp.bfloat16)
    low = (value - high.astype(jnp.float32)).astype(jnp.bfloat16)
    return high, low


def column_sums(value):
    return jnp.sum(value, axis=1, keepdims=True)


def fused(
    depth,
    points_hbm, targets_hbm, lengths_hbm, scale_ref, noise_ref,
    solution_ref, residual_ref,
    stack, images, kern_high, kern_low, parts, landing, scalars,
    points_ref, targets_ref, lengths_ref, load_sem,
    send_a, recv_a, send_b, recv_b, send_p, recv_p, send_s, recv_s,
):
    features, local = points_ref.shape
    rhs = targets_ref.shape[0]
    pairs = ((points_hbm, points_ref), (targets_hbm, targets_ref), (lengths_hbm, lengths_ref))
    loads = [
        pltpu.make_async_copy(source, target, load_sem.at[at])
        for at, (source, target) in enumerate(pairs)
    ]
    for load in loads:
        load.start()
    wide, row = lax.axis_index("wide"), lax.axis_index("row")
    core = lax.rem(wide, CORES)
    x = lax.rem(lax.div(wide, CORES), SIDE)
    z = lax.div(wide, CORES * SIDE)
    plane = [(dx, dy, dc) for dc in range(CORES) for dx in range(SIDE) for dy in range(SIDE)]
    across = [(dx, dy, 0) for dx in range(SIDE) for dy in range(SIDE) if dx + dy > 0]
    width = len(plane)
    everyone = [(level, *at) for level in range(depth) for at in plane][1:]

    def place(level, dx, dy, dc):
        at_z, at_x, at_y, at_c = flip(z, level), flip(x, dx), flip(row, dy), flip(core, dc)
        return ((at_z * SIDE + at_x) * CORES + at_c, at_y)

    def number(dx, dy, dc):
        return plane.index((dx, dy, dc))

    barrier = pltpu.get_barrier_semaphore()
    for peer in everyone:
        pl.semaphore_signal(barrier, inc=1, device_id=place(*peer), device_id_type=MESH)

    for load in loads:
        load.wait()
    lengths = jnp.broadcast_to(lengths_ref[...], (features, features)).T
    targets = targets_ref[...]
    stack[0, :features, :] = points_ref[...] / lengths[:, :local]
    stack[0, features:, :] = targets
    images[0] = jnp.zeros_like(targets)
    pl.semaphore_wait(barrier, len(everyone))

    started = []

    def copy(source, target, sends, sent, recvs, received, to):
        made = pltpu.make_async_remote_copy(
            src_ref=source,
            dst_ref=target,
            send_sem=sends.at[sent],
            recv_sem=recvs.at[received],
            device_id=place(*to),
            device_id_type=MESH,
        )
        made.start()
        started.append(made)
        return made

    def spread(buffer, sends, recvs):
        column, beside = {}, {}
        for level in range(1, depth):
            at = width + level - 1
            column[level] = copy(buffer.at[0], buffer.at[at], sends, at, recvs, at, (level, 0, 0, 0))
        for to in across:
            at = number(*to)
            beside[to] = copy(buffer.at[0], buffer.at[at], sends, at, recvs, at, (0, *to))
        at = number(0, 0, 1)
        beside[0, 0, 1] = copy(buffer.at[0], buffer.at[at], sends, at, recvs, at, (0, 0, 0, 1))
        return column, beside

    def relay(buffer, sends, recvs, beside):
        for to in across:
            beside[to].wait_recv()
            at = number(to[0], to[1], 1)
            beside[to[0], to[1], 1] = copy(
                buffer.at[number(*to)], buffer.at[at], sends, at, recvs, at, (0, 0, 0, 1)
            )
        for at in plane[SIDE * SIDE :]:
            beside[at].wait_recv()

    kern_scale = scale_ref[0]
    noise_var = noise_ref[0]

    def apply(vectors, level):
        total = None
        for at, (vec_high, vec_low) in enumerate(vectors):
            tile_high, tile_low = kern_high[level * width + at], kern_low[level * width + at]
            part = lax.dot_general(
                jnp.concatenate([vec_high, vec_low], axis=1),
                jnp.concatenate([tile_high, tile_high], axis=1),
                (((1,), (1,)), ((), ())),
                preferred_element_type=jnp.float32,
            ) + lax.dot_general(
                vec_high, tile_low, (((1,), (1,)), ((), ())), preferred_element_type=jnp.float32
            )
            total = part if total is None else total + part
        return total

    def build(level):
        own = stack[0 if level == 0 else width + level - 1, :features, :].T
        own_sq = column_sums(own * own)
        high, low = halves(own)
        left = jnp.concatenate(
            [jnp.concatenate([high, high], axis=1), jnp.concatenate([low, low], axis=1)], axis=0
        )
        for at in range(width):
            block = stack[at, :features, :]
            block_high, block_low = halves(block)
            product = jnp.dot(
                left,
                jnp.concatenate([block_high, block_low], axis=0),
                preferred_element_type=jnp.float32,
            )
            cross = product[:local] + product[local:]
            block_sq = jnp.sum(block * block, axis=0, keepdims=True)
            tile = kern_scale * jnp.exp(-0.5 * (own_sq + block_sq - 2.0 * cross))
            tile_high, tile_low = halves(tile)
            kern_high[level * width + at] = tile_high
            kern_low[level * width + at] = tile_low

    def send_part(turn, level, value):
        at = turn * depth + level
        parts[at] = value
        return copy(parts.at[at], landing.at[at], send_p, at, recv_p, at, (level, 0, 0, 0))

    def send_scalars(turn, values):
        pad = jnp.zeros((local - len(values) * rhs, local), jnp.float32)
        sums = jnp.sum(jnp.concatenate([*values, pad], axis=0).T, axis=0, keepdims=True)
        base = turn * (len(everyone) + 1)
        scalars[base] = jnp.broadcast_to(sums, scalars.shape[1:])
        return [
            copy(scalars.at[base], scalars.at[base + 1 + at], send_s, base + 1 + at, recv_s, base + 1 + at, peer)
            for at, peer in enumerate(everyone)
        ]

    def all_scalars(turn, copies):
        for one in copies:
            one.wait_recv()
        base = turn * (len(everyone) + 1)
        total = scalars[base]
        for at in range(len(everyone)):
            total = total + scalars[base + 1 + at]
        return jnp.broadcast_to(total[:1], (local, local)).T

    column, beside = spread(stack, send_a, recv_a)
    relay(stack, send_a, recv_a, beside)
    vectors = [halves(stack[at, features:, :]) for at in range(width)]
    build(0)
    mine = apply(vectors, 0)
    sent = []
    for level in range(1, depth):
        column[level].wait_recv()
        build(level)
        sent.append(send_part(0, level, apply(vectors, level)))
    for one in sent:
        one.wait_recv()
    for level in range(1, depth):
        mine = mine + landing[level]
    first_image = mine + noise_var * targets
    images[0] = first_image
    column, beside = spread(images, send_b, recv_b)
    sent = send_scalars(0, [targets * targets, targets * first_image, first_image * first_image])
    relay(images, send_b, recv_b, beside)
    for level in range(1, depth):
        column[level].wait_recv()
    found = all_scalars(0, sent)
    norm_now, curve, image_sq = found[:rhs], found[rhs : 2 * rhs], found[2 * rhs : 3 * rhs]
    step = norm_now / curve
    norm_next = norm_now - 2.0 * step * curve + step * step * image_sq
    ratio = norm_next / norm_now

    def turned(at):
        vector = stack[at, features:, :]
        return (vector - step * images[at]) + ratio * vector

    vectors = [halves(turned(at)) for at in range(width)]
    direction = turned(0)
    sent = []
    weighted = noise_var * direction * direction
    for level in range(1, depth):
        part = apply(vectors, level)
        sent.append(send_part(1, level, part))
        weighted += turned(width + level - 1) * part
    mine = apply(vectors, 0)
    weighted += direction * mine
    sums = send_scalars(1, [weighted])
    for one in sent:
        one.wait_recv()
    for level in range(1, depth):
        mine = mine + landing[depth + level]
    image = mine + noise_var * direction
    residual = targets - step * first_image
    last_step = norm_next / all_scalars(1, sums)[:rhs]
    solution_ref[...] = step * targets + last_step * direction
    residual_ref[...] = residual - last_step * image
    for one in started:
        one.wait_send()


def on_device_fused(points, targets, lengthscales, outputscale, noise):
    features, local = points.shape
    rhs = targets.shape[0]
    devices = lax.axis_size("wide") * lax.axis_size("row")
    depth = lax.axis_size("wide") // (CORES * SIDE)
    vmem, smem = pl.BlockSpec(memory_space=pltpu.VMEM), pl.BlockSpec(memory_space=pltpu.SMEM)
    hbm = pl.BlockSpec(memory_space=pltpu.HBM)
    own = jax.ShapeDtypeStruct((rhs, local), jnp.float32)
    width = SIDE * SIDE * CORES
    near = width + depth - 1
    dma = pltpu.SemaphoreType.DMA
    return pl.pallas_call(
        functools.partial(fused, depth),
        out_shape=(own, own),
        in_specs=[hbm, hbm, hbm, smem, smem],
        out_specs=(vmem, vmem),
        scratch_shapes=[
            pltpu.VMEM((near, features + rhs, local), jnp.float32),
            pltpu.VMEM((near, rhs, local), jnp.float32),
            pltpu.VMEM((depth * width, local, local), jnp.bfloat16),
            pltpu.VMEM((depth * width, local, local), jnp.bfloat16),
            pltpu.VMEM((2 * depth, rhs, local), jnp.float32),
            pltpu.VMEM((2 * depth, rhs, local), jnp.float32),
            pltpu.VMEM((2 * devices, 1, local), jnp.float32),
            pltpu.VMEM((features, local), jnp.float32),
            pltpu.VMEM((rhs, local), jnp.float32),
            pltpu.VMEM((1, features), jnp.float32),
            dma((3,)),
            dma((near,)),
            dma((near,)),
            dma((near,)),
            dma((near,)),
            dma((2 * depth,)),
            dma((2 * depth,)),
            dma((2 * devices,)),
            dma((2 * devices,)),
        ],
        compiler_params=pltpu.CompilerParams(
            collective_id=0, has_side_effects=True, vmem_limit_bytes=VMEM_BUDGET
        ),
    )(points, targets, lengthscales[None, :], outputscale, noise)


def solution(mesh):
    sizes = dict(mesh.shape)
    devices = sizes["wide"] * sizes["row"]
    depth = sizes["wide"] // (CORES * SIDE)

    def whole(points, targets, lengthscales, outputscale, noise):
        features, count = points.shape
        rhs = targets.shape[0]
        local = count // devices
        held = 4 * count * (features + 3 * rhs + local)
        fits = (
            sizes["row"] == SIDE
            and sizes["wide"] == depth * CORES * SIDE
            and depth & (depth - 1) == 0
            and local == features
            and 3 * rhs <= local
            and 2 * held <= VMEM_BUDGET
        )
        own = P(None, ("wide", "row"))
        return jax.shard_map(
            on_device_fused if fits else on_device,
            mesh=mesh,
            in_specs=(own, own, P(), P(), P()),
            out_specs=(own, own),
            check_vma=False,
        )(points, targets, lengthscales, outputscale, noise)

    return whole
```

```python
import functools

import jax
import jax.numpy as jnp
from jax import lax
from jax.experimental import pallas as pl
from jax.experimental.pallas import tpu as pltpu
from jax.sharding import PartitionSpec as P

ITERS = 2


def from_behind(value, axis, steps):
    count = lax.axis_size(axis)
    pairs = [(source, (source + steps) % count) for source in range(count)]
    return lax.ppermute(value, axis, pairs)


def kernel_tile(left_pts, left_sq, right_pts, right_sq, kern_scale):
    cross = lax.dot_general(
        left_pts, right_pts, (((0,), (0,)), ((), ())), precision=lax.Precision.HIGHEST
    )
    distance = left_sq[:, None] + right_sq[None, :] - 2.0 * cross
    return kern_scale * jnp.exp(-0.5 * distance)


def apply_rows(vectors, kernel):
    return lax.dot_general(
        vectors, kernel, (((1,), (1,)), ((), ())), precision=lax.Precision.HIGHEST
    )


def apply_columns(vectors, kernel):
    return lax.dot_general(
        vectors, kernel, (((1,), (0,)), ((), ())), precision=lax.Precision.HIGHEST
    )


def on_device(points, targets, lengthscales, outputscale, noise):
    wide_count = lax.axis_size("wide")
    row_count = lax.axis_size("row")
    half_cycle = wide_count // 2
    slot_count = half_cycle // row_count
    member = lax.axis_index("row")
    scaled = points / lengthscales[:, None]
    kern_scale = outputscale[0]
    noise_var = noise[0]
    features = scaled.shape[0]
    local_count = points.shape[1]

    def collect(stacked):
        window = stacked[None]
        while window.shape[0] < half_cycle:
            arrived = from_behind(window, "wide", -window.shape[0])
            window = jnp.concatenate([window, arrived], axis=0)
        return window

    def assemble(stacked):
        across = from_behind(stacked, "wide", -half_cycle)
        table = collect(stacked)
        channels = table.shape[1]
        nearer = table.reshape(slot_count, row_count, channels, local_count).transpose(0, 2, 1, 3)
        own_block = jnp.broadcast_to(
            table[0][None, :, None, :], (1, channels, row_count, local_count)
        )
        outgoing = jnp.concatenate([own_block, nearer], axis=0)
        arrived = lax.all_to_all(outgoing, "row", split_axis=2, concat_axis=2, tiled=True)
        return (arrived.reshape(slot_count + 1, channels, row_count * local_count), across)

    solution = jnp.zeros_like(targets)
    residual = targets
    direction = targets
    norm_now = lax.psum(jnp.sum(residual * residual, axis=1), ("wide", "row"))
    cache = None
    for iteration in range(ITERS):
        operate_cache = cache
        if operate_cache is None:
            blocks, operate_across = assemble(jnp.concatenate([scaled, direction], axis=0))
            point_blocks = blocks[:, :features]
            vector_blocks = blocks[:, features:]
            far_points = operate_across[:features]
            far_vector = operate_across[features:]
            operate_cache = (
                point_blocks,
                jnp.sum(point_blocks * point_blocks, axis=1),
                far_points,
                jnp.sum(far_points * far_points, axis=0),
            )
        else:
            vector_blocks, far_vector = assemble(direction)
        point_blocks, block_sq, far_points, far_sq = operate_cache
        left_pts = point_blocks[0]
        left_sq = block_sq[0]
        left_vec = vector_blocks[0]
        kernel = kernel_tile(left_pts, left_sq, far_points, far_sq, kern_scale)
        own_rows = apply_rows(far_vector, kernel)
        operate_partials = []
        for slot_index in range(slot_count):
            kernel = kernel_tile(
                left_pts,
                left_sq,
                point_blocks[slot_index + 1],
                block_sq[slot_index + 1],
                kern_scale,
            )
            own_rows = own_rows + apply_rows(vector_blocks[slot_index + 1], kernel)
            weight = (member + row_count * slot_index != 0).astype(jnp.float32)
            operate_partials.append(weight * apply_columns(left_vec, kernel))
        partials = jnp.stack([own_rows] + operate_partials, axis=0)
        rhs_count = partials.shape[1]
        pieces = partials.reshape(slot_count + 1, rhs_count, row_count, local_count)
        spread_arrived = lax.all_to_all(pieces, "row", split_axis=2, concat_axis=2, tiled=True)
        mine = jnp.sum(spread_arrived[0], axis=1)
        by_distance = (
            spread_arrived[1:].transpose(0, 2, 1, 3).reshape(half_cycle, rhs_count, local_count)
        )
        by_distance = by_distance.at[0].add(mine)
        held = by_distance
        span_size = half_cycle
        while span_size > 1:
            span_size = span_size // 2
            held = held[:span_size] + from_behind(held[span_size:], "wide", span_size)
        summed = held[0]
        image = summed + noise_var * direction
        cache = operate_cache
        curve, cross_term, image_sq = lax.psum(
            (
                jnp.sum(direction * image, axis=1),
                jnp.sum(residual * image, axis=1),
                jnp.sum(image * image, axis=1),
            ),
            ("wide", "row"),
        )
        step_size = norm_now / curve
        norm_next = norm_now - 2.0 * step_size * cross_term + step_size * step_size * image_sq
        solution = solution + step_size[:, None] * direction
        residual = residual - step_size[:, None] * image
        if iteration + 1 < ITERS:
            direction = residual + (norm_next / norm_now)[:, None] * direction
            norm_now = norm_next
    return (solution, residual)


MESH = pl.DeviceIdType.MESH
VMEM_BUDGET = 48 * 2**20
CORES = 2
SIDE = 2


def flip(index, mask):
    bit = 1
    while bit <= mask:
        if mask & bit:
            index = index + bit - 2 * bit * lax.rem(lax.div(index, bit), 2)
        bit *= 2
    return index


def halves(value):
    high = value.astype(jnp.bfloat16)
    low = (value - high.astype(jnp.float32)).astype(jnp.bfloat16)
    return high, low


def column_sums(value):
    return jnp.sum(value, axis=1, keepdims=True)


def fused(
    depth,
    points_hbm, targets_hbm, lengths_hbm, scale_ref, noise_ref,
    solution_ref, residual_ref,
    stack, images, kern_high, kern_low, parts, landing, scalars,
    points_ref, targets_ref, lengths_ref, load_sem,
    send_a, recv_a, send_b, recv_b, send_p, recv_p, send_s, recv_s,
):
    features, local = points_ref.shape
    rhs = targets_ref.shape[0]
    pairs = ((points_hbm, points_ref), (targets_hbm, targets_ref), (lengths_hbm, lengths_ref))
    loads = [
        pltpu.make_async_copy(source, target, load_sem.at[at])
        for at, (source, target) in enumerate(pairs)
    ]
    for load in loads:
        load.start()
    wide, row = lax.axis_index("wide"), lax.axis_index("row")
    core = lax.rem(wide, CORES)
    x = lax.rem(lax.div(wide, CORES), SIDE)
    z = lax.div(wide, CORES * SIDE)
    plane = [(dx, dy, dc) for dc in range(CORES) for dx in range(SIDE) for dy in range(SIDE)]
    across = [(dx, dy, 0) for dx in range(SIDE) for dy in range(SIDE) if dx + dy > 0]
    width = len(plane)
    everyone = [(level, *at) for level in range(depth) for at in plane][1:]

    def place(level, dx, dy, dc):
        at_z, at_x, at_y, at_c = flip(z, level), flip(x, dx), flip(row, dy), flip(core, dc)
        return ((at_z * SIDE + at_x) * CORES + at_c, at_y)

    def number(dx, dy, dc):
        return plane.index((dx, dy, dc))

    barrier = pltpu.get_barrier_semaphore()
    for peer in everyone:
        pl.semaphore_signal(barrier, inc=1, device_id=place(*peer), device_id_type=MESH)

    for load in loads:
        load.wait()
    lengths = jnp.broadcast_to(lengths_ref[...], (features, features)).T
    targets = targets_ref[...]
    stack[0, :features, :] = points_ref[...] / lengths[:, :local]
    stack[0, features:, :] = targets
    images[0] = jnp.zeros_like(targets)
    pl.semaphore_wait(barrier, len(everyone))

    started = []

    def copy(source, target, sends, sent, recvs, received, to):
        made = pltpu.make_async_remote_copy(
            src_ref=source,
            dst_ref=target,
            send_sem=sends.at[sent],
            recv_sem=recvs.at[received],
            device_id=place(*to),
            device_id_type=MESH,
        )
        made.start()
        started.append(made)
        return made

    def spread(buffer, sends, recvs):
        column, beside = {}, {}
        for level in range(1, depth):
            at = width + level - 1
            column[level] = copy(buffer.at[0], buffer.at[at], sends, at, recvs, at, (level, 0, 0, 0))
        for to in across:
            at = number(*to)
            beside[to] = copy(buffer.at[0], buffer.at[at], sends, at, recvs, at, (0, *to))
        at = number(0, 0, 1)
        beside[0, 0, 1] = copy(buffer.at[0], buffer.at[at], sends, at, recvs, at, (0, 0, 0, 1))
        return column, beside

    def relay(buffer, sends, recvs, beside):
        for to in across:
            beside[to].wait_recv()
            at = number(to[0], to[1], 1)
            beside[to[0], to[1], 1] = copy(
                buffer.at[number(*to)], buffer.at[at], sends, at, recvs, at, (0, 0, 0, 1)
            )
        for at in plane[SIDE * SIDE :]:
            beside[at].wait_recv()

    kern_scale = scale_ref[0]
    noise_var = noise_ref[0]

    def apply(vectors, level):
        total = None
        for at, (vec_high, vec_low) in enumerate(vectors):
            tile_high, tile_low = kern_high[level * width + at], kern_low[level * width + at]
            part = lax.dot_general(
                jnp.concatenate([vec_high, vec_low], axis=1),
                jnp.concatenate([tile_high, tile_high], axis=1),
                (((1,), (1,)), ((), ())),
                preferred_element_type=jnp.float32,
            ) + lax.dot_general(
                vec_high, tile_low, (((1,), (1,)), ((), ())), preferred_element_type=jnp.float32
            )
            total = part if total is None else total + part
        return total

    def build(level):
        own = stack[0 if level == 0 else width + level - 1, :features, :].T
        own_sq = column_sums(own * own)
        high, low = halves(own)
        left = jnp.concatenate(
            [jnp.concatenate([high, high], axis=1), jnp.concatenate([low, low], axis=1)], axis=0
        )
        for at in range(width):
            block = stack[at, :features, :]
            block_high, block_low = halves(block)
            product = jnp.dot(
                left,
                jnp.concatenate([block_high, block_low], axis=0),
                preferred_element_type=jnp.float32,
            )
            cross = product[:local] + product[local:]
            block_sq = jnp.sum(block * block, axis=0, keepdims=True)
            tile = kern_scale * jnp.exp(-0.5 * (own_sq + block_sq - 2.0 * cross))
            tile_high, tile_low = halves(tile)
            kern_high[level * width + at] = tile_high
            kern_low[level * width + at] = tile_low

    def send_part(turn, level, value):
        at = turn * depth + level
        parts[at] = value
        return copy(parts.at[at], landing.at[at], send_p, at, recv_p, at, (level, 0, 0, 0))

    def send_scalars(turn, values):
        pad = jnp.zeros((local - len(values) * rhs, local), jnp.float32)
        sums = jnp.sum(jnp.concatenate([*values, pad], axis=0).T, axis=0, keepdims=True)
        base = turn * (len(everyone) + 1)
        scalars[base] = jnp.broadcast_to(sums, scalars.shape[1:])
        return [
            copy(scalars.at[base], scalars.at[base + 1 + at], send_s, base + 1 + at, recv_s, base + 1 + at, peer)
            for at, peer in enumerate(everyone)
        ]

    def all_scalars(turn, copies):
        for one in copies:
            one.wait_recv()
        base = turn * (len(everyone) + 1)
        total = scalars[base]
        for at in range(len(everyone)):
            total = total + scalars[base + 1 + at]
        return jnp.broadcast_to(total[:1], (local, local)).T

    column, beside = spread(stack, send_a, recv_a)
    relay(stack, send_a, recv_a, beside)
    vectors = [halves(stack[at, features:, :]) for at in range(width)]
    build(0)
    mine = apply(vectors, 0)
    sent = []
    for level in range(1, depth):
        column[level].wait_recv()
        build(level)
        sent.append(send_part(0, level, apply(vectors, level)))
    for one in sent:
        one.wait_recv()
    for level in range(1, depth):
        mine = mine + landing[level]
    first_image = mine + noise_var * targets
    images[0] = first_image
    column, beside = spread(images, send_b, recv_b)
    for to in across:
        far = (to[0], to[1], 1)
        at = number(*far)
        beside[far] = copy(images.at[0], images.at[at], send_b, at, recv_b, at, (0, *far))
    sent = send_scalars(0, [targets * targets, targets * first_image, first_image * first_image])
    for at in plane[1:]:
        beside[at].wait_recv()
    for level in range(1, depth):
        column[level].wait_recv()
    found = all_scalars(0, sent)
    norm_now, curve, image_sq = found[:rhs], found[rhs : 2 * rhs], found[2 * rhs : 3 * rhs]
    step = norm_now / curve
    norm_next = norm_now - 2.0 * step * curve + step * step * image_sq
    ratio = norm_next / norm_now

    def turned(at):
        vector = stack[at, features:, :]
        return (vector - step * images[at]) + ratio * vector

    vectors = [halves(turned(at)) for at in range(width)]
    direction = turned(0)
    sent = []
    weighted = noise_var * direction * direction
    for level in range(1, depth):
        part = apply(vectors, level)
        sent.append(send_part(1, level, part))
        weighted += turned(width + level - 1) * part
    mine = apply(vectors, 0)
    weighted += direction * mine
    sums = send_scalars(1, [weighted])
    for one in sent:
        one.wait_recv()
    for level in range(1, depth):
        mine = mine + landing[depth + level]
    image = mine + noise_var * direction
    residual = targets - step * first_image
    last_step = norm_next / all_scalars(1, sums)[:rhs]
    solution_ref[...] = step * targets + last_step * direction
    residual_ref[...] = residual - last_step * image
    for one in started:
        one.wait_send()


def on_device_fused(points, targets, lengthscales, outputscale, noise):
    features, local = points.shape
    rhs = targets.shape[0]
    devices = lax.axis_size("wide") * lax.axis_size("row")
    depth = lax.axis_size("wide") // (CORES * SIDE)
    vmem, smem = pl.BlockSpec(memory_space=pltpu.VMEM), pl.BlockSpec(memory_space=pltpu.SMEM)
    hbm = pl.BlockSpec(memory_space=pltpu.HBM)
    own = jax.ShapeDtypeStruct((rhs, local), jnp.float32)
    width = SIDE * SIDE * CORES
    near = width + depth - 1
    dma = pltpu.SemaphoreType.DMA
    return pl.pallas_call(
        functools.partial(fused, depth),
        out_shape=(own, own),
        in_specs=[hbm, hbm, hbm, smem, smem],
        out_specs=(vmem, vmem),
        scratch_shapes=[
            pltpu.VMEM((near, features + rhs, local), jnp.float32),
            pltpu.VMEM((near, rhs, local), jnp.float32),
            pltpu.VMEM((depth * width, local, local), jnp.bfloat16),
            pltpu.VMEM((depth * width, local, local), jnp.bfloat16),
            pltpu.VMEM((2 * depth, rhs, local), jnp.float32),
            pltpu.VMEM((2 * depth, rhs, local), jnp.float32),
            pltpu.VMEM((2 * devices, 1, local), jnp.float32),
            pltpu.VMEM((features, local), jnp.float32),
            pltpu.VMEM((rhs, local), jnp.float32),
            pltpu.VMEM((1, features), jnp.float32),
            dma((3,)),
            dma((near,)),
            dma((near,)),
            dma((near,)),
            dma((near,)),
            dma((2 * depth,)),
            dma((2 * depth,)),
            dma((2 * devices,)),
            dma((2 * devices,)),
        ],
        compiler_params=pltpu.CompilerParams(
            collective_id=0, has_side_effects=True, vmem_limit_bytes=VMEM_BUDGET
        ),
    )(points, targets, lengthscales[None, :], outputscale, noise)


def solution(mesh):
    sizes = dict(mesh.shape)
    devices = sizes["wide"] * sizes["row"]
    depth = sizes["wide"] // (CORES * SIDE)

    def whole(points, targets, lengthscales, outputscale, noise):
        features, count = points.shape
        rhs = targets.shape[0]
        local = count // devices
        held = 4 * count * (features + 3 * rhs + local)
        fits = (
            sizes["row"] == SIDE
            and sizes["wide"] == depth * CORES * SIDE
            and depth & (depth - 1) == 0
            and local == features
            and 3 * rhs <= local
            and 2 * held <= VMEM_BUDGET
        )
        own = P(None, ("wide", "row"))
        return jax.shard_map(
            on_device_fused if fits else on_device,
            mesh=mesh,
            in_specs=(own, own, P(), P(), P()),
            out_specs=(own, own),
            check_vma=False,
        )(points, targets, lengthscales, outputscale, noise)

    return whole
```
